32 devices in a mesh: rows: 16 (over z, y, x), layers: 2 (over core).
Axes of the slice: x: 2, y: 2, z: 4, core: 2. Of those that a mesh axis runs over, the one named last changes fastest.
Arguments:
- panel: float32 [8, 4096, 1024], P('layers', 'rows'), may hold values from -6 to 6, as said below
- factor: float32 [8, 4096, 2048], P(None, 'rows', 'layers'), may hold values from -4 to 4
Outputs:
- solved: float32 [8, 4096, 1024], P('layers', 'rows')
The draws below stay inside these ranges and needn't reach their ends.
Inputs may be any that keep to these rules, and one draw needn't show every extreme that they name: The first 1024 rows of panel minus those rows of factor times the transpose of the first 1024 rows of factor form a symmetric positive definite block whose smallest eigenvalue is above 0.4.
All inputs are finite; a program needn't handle non-finite values.
Results may differ from the reference program's by a relative error of at most 0.00024.
Values sent between devices are 32-bit elements; how exact they have to be, the bound alone decides.
A program may use at most 128 MiB of HBM per device.

```python
import math
import jax
import jax.numpy as jnp
from jax import lax

NB = 1024
RB = 256
CYCLES = 8
K = 2048
N_ROWS = 16


def factor_values(key, count, scale):
    return jax.random.truncated_normal(key, -4.0, 4.0, (count, K), jnp.float32) * scale


def head_values(key):
    return factor_values(jax.random.fold_in(key, 100), NB, 0.5 * K ** (-0.5))


def draw_factor(key, part):
    total_rows = CYCLES * N_ROWS * RB
    head_rows = head_values(key)
    tail_rows = factor_values(jax.random.fold_in(key, 101), total_rows - NB, 1.0)
    return jnp.concatenate([head_rows, tail_rows], 0).reshape(CYCLES, N_ROWS * RB, K)


def draw_panel(key, part):
    total_rows = CYCLES * N_ROWS * RB
    head_rows = head_values(key)
    keys = jax.random.split(jax.random.fold_in(key, 200), 3)
    mixing = jax.random.normal(keys[0], (NB, NB), jnp.float32)
    scales = jnp.exp(jax.random.uniform(keys[1], (NB,), jnp.float32, math.log(0.6), math.log(1.6)))
    coupling = jnp.dot(mixing, mixing.T, precision=lax.Precision.HIGHEST, preferred_element_type=jnp.float32)
    coupling = (coupling + coupling.T) * (0.25 / NB)
    positions = jnp.arange(NB, dtype=jnp.float32)
    distance = jnp.abs(positions[:, None] - positions[None, :])
    kernel = jnp.exp(-distance / 16.0) * scales[:, None] * scales[None, :]
    block = coupling + kernel + 0.5 * jnp.eye(NB, dtype=jnp.float32)
    block = block + jnp.dot(head_rows, head_rows.T, precision=lax.Precision.HIGHEST, preferred_element_type=jnp.float32)
    rest_rows = jax.random.truncated_normal(keys[2], -6.0, 6.0, (total_rows - NB, NB), jnp.float32)
    return jnp.concatenate([block, rest_rows], 0).reshape(CYCLES, N_ROWS * RB, NB)


def setup_inputs(seed: int = 0) -> dict:
    key_of = jax.random.split(jax.random.key(seed), 3)
    return {
        "panel": draw_panel(jax.random.fold_in(key_of[2], 71), 0),
        "factor": draw_factor(jax.random.fold_in(key_of[2], 71), 0),
    }


def reference(panel, factor):
    panel_rows = panel.reshape(-1, NB)
    factor_rows = factor.reshape(-1, K)
    target = factor_rows[:NB]
    update = jnp.dot(factor_rows.astype(jnp.float32), target.T.astype(jnp.float32), precision=lax.Precision.HIGHEST, preferred_element_type=jnp.float32)
    reduced = panel_rows - update
    diag_factor = jnp.linalg.cholesky(reduced[:NB])
    solved = jax.scipy.linalg.solve_triangular(diag_factor, reduced.T, lower=True).T
    return solved.reshape(panel.shape)
```

```python
import functools
import jax
import jax.numpy as jnp
from jax import lax
from jax.experimental import pallas as pl
from jax.experimental.pallas import tpu as pltpu
from jax.sharding import PartitionSpec as P

MESH = pl.DeviceIdType.MESH
HIGH = lax.Precision.HIGH
TILE = 128
CHUNKS = 4


def gather_kernel(groups, peers, f_ref, p_ref, t_ref, d_ref, local_sem, z_send, z_recv, g_send, g_recv):
    row = lax.axis_index("rows")
    layer = lax.axis_index("layers")
    group = row // peers
    place = lax.rem(row, peers)
    base = group * peers
    has_prev = group > 0
    has_next = group < groups - 1
    prev = jnp.where(has_prev, row - peers, row)
    following = jnp.where(has_next, row + peers, row)
    size = f_ref.shape[0]
    part = size // CHUNKS

    barrier = pltpu.get_barrier_semaphore()

    def greet(who):
        pl.semaphore_signal(barrier, inc=1, device_id=(who, layer), device_id_type=MESH)

    for k in range(1, peers):
        greet(base + lax.rem(place + k, peers))

    @pl.when(has_prev)
    def _():
        greet(prev)

    @pl.when(has_next)
    def _():
        greet(following)

    pl.semaphore_wait(barrier, peers - 1 + has_prev.astype(jnp.int32) + has_next.astype(jnp.int32))

    def rows_of(owner, c):
        return pl.ds(pl.multiple_of(owner * size + c * part, part), part)

    def chain(a, dst, c):
        return pltpu.make_async_remote_copy(
            src_ref=dst.at[rows_of(place, c)], dst_ref=dst.at[rows_of(place, c)],
            send_sem=z_send.at[a, c], recv_sem=z_recv.at[a, c],
            device_id=(following, layer), device_id_type=MESH)

    def spread(a, dst, c, k):
        to = base + lax.rem(place + k, peers)
        return pltpu.make_async_remote_copy(
            src_ref=dst.at[rows_of(place, c)], dst_ref=dst.at[rows_of(place, c)],
            send_sem=g_send.at[a, c, k], recv_sem=g_recv.at[a, c, k],
            device_id=(to, layer), device_id_type=MESH)

    def arrival(a, dst, c, k):
        src = lax.rem(place + peers - k, peers)
        return pltpu.make_async_remote_copy(
            src_ref=dst.at[rows_of(src, c)], dst_ref=dst.at[rows_of(src, c)],
            send_sem=g_send.at[a, c, k], recv_sem=g_recv.at[a, c, k],
            device_id=(base + src, layer), device_id_type=MESH)

    def each(body):
        body(0, f_ref, t_ref)

        @pl.when(layer == 0)
        def _():
            body(1, p_ref, d_ref)

    def own(a, src, dst):
        return pltpu.make_async_copy(src, dst.at[pl.ds(pl.multiple_of(place * size, size), size)], local_sem.at[a])

    @pl.when(jnp.logical_not(has_prev))
    def _():
        each(lambda a, src, dst: own(a, src, dst).start())
        each(lambda a, src, dst: own(a, src, dst).wait())

    for c in range(CHUNKS):
        def step(a, src, dst):
            @pl.when(has_prev)
            def _():
                chain(a, dst, c).wait_recv()

            @pl.when(has_next)
            def _():
                chain(a, dst, c).start()

            for k in range(1, peers):
                spread(a, dst, c, k).start()

        each(step)

    for c in range(CHUNKS):
        def finish(a, src, dst):
            for k in range(1, peers):
                arrival(a, dst, c, k).wait_recv()
                spread(a, dst, c, k).wait_send()

            @pl.when(has_next)
            def _():
                chain(a, dst, c).wait_send()

        each(finish)


def gather(groups, peers, f, p):
    rows, cols = f.shape
    out = jax.ShapeDtypeStruct((peers * rows, cols), f.dtype)
    out_p = jax.ShapeDtypeStruct((peers * rows, p.shape[1]), p.dtype)
    dma = pltpu.SemaphoreType.DMA
    return pl.pallas_call(
        functools.partial(gather_kernel, groups, peers),
        out_shape=(out, out_p),
        in_specs=[pl.BlockSpec(memory_space=pl.ANY)] * 2,
        out_specs=(pl.BlockSpec(memory_space=pl.ANY),) * 2,
        scratch_shapes=[dma((2,)), dma((2, CHUNKS)), dma((2, CHUNKS)),
                        dma((2, CHUNKS, peers)), dma((2, CHUNKS, peers))],
        compiler_params=pltpu.CompilerParams(collective_id=0, has_side_effects=True),
    )(f, p)


def split(x):
    hi = x.astype(jnp.bfloat16)
    return hi, (x - hi.astype(jnp.float32)).astype(jnp.bfloat16)


def dot3(a, b):
    a_hi, a_lo = a
    b_hi, b_lo = b
    mm = functools.partial(jnp.dot, preferred_element_type=jnp.float32)
    return mm(a_hi, b_hi) + (mm(a_hi, b_lo) + mm(a_lo, b_hi))


def base_inverse(block):
    n = TILE // 8
    sub = lax.broadcasted_iota(jnp.int32, (8, TILE), 0)
    lane = lax.broadcasted_iota(jnp.int32, (8, TILE), 1)
    a = [block[8 * i:8 * i + 8, :] for i in range(n)]
    x = [jnp.where(lane == sub + 8 * i, 1.0, 0.0).astype(jnp.float32) for i in range(n)]
    for j in range(TILE):
        s, o = j // 8, j % 8
        row = jnp.broadcast_to(a[s][o:o + 1, :], (8, TILE))
        root = lax.rsqrt(jnp.broadcast_to(row[:, j:j + 1], (8, TILE)))
        row = row * root
        xrow = jnp.broadcast_to(x[s][o:o + 1, :], (8, TILE)) * root
        for i in range(s, n):
            col = jnp.broadcast_to(a[i][:, j:j + 1], (8, TILE)) * root
            if i == s:
                x[i] = jnp.where(sub == o, xrow, jnp.where(sub > o, x[i] - col * xrow, x[i]))
                a[i] = a[i] - jnp.where(sub > o, col, 0.0) * row
            else:
                a[i] = a[i] - col * row
                x[i] = x[i] - col * xrow
    return jnp.concatenate(x, 0)


def inverse_kernel(d_ref, o_ref, m_ref):
    size = d_ref.shape[0]
    count = size // TILE
    m_ref[...] = d_ref[...]
    col_tile = lax.broadcasted_iota(jnp.int32, (TILE, size), 1) // TILE
    eye = (lax.broadcasted_iota(jnp.int32, (TILE, TILE), 0)
           == lax.broadcasted_iota(jnp.int32, (TILE, TILE), 1)).astype(jnp.float32)

    @pl.loop(0, count)
    def _(b):
        here = pl.ds(pl.multiple_of(b * TILE, TILE), TILE)
        inv = base_inverse(m_ref[here, here])
        m_ref[here, here] = eye
        u = dot3(split(inv), split(m_ref[here, :]))
        o_ref[here, :] = jnp.where(col_tile <= b, u, 0.0)
        m_ref[here, :] = u
        u_parts = split(u)

        @pl.loop(b + 1, count)
        def _(i):
            there = pl.ds(pl.multiple_of(i * TILE, TILE), TILE)
            left = m_ref[here, there].T
            old = jnp.where(col_tile == b, 0.0, m_ref[there, :])
            m_ref[there, :] = old - dot3(split(left), u_parts)


def factor_inverse(d):
    size = d.shape[0]
    return pl.pallas_call(
        inverse_kernel,
        out_shape=jax.ShapeDtypeStruct((size, size), jnp.float32),
        in_specs=[pl.BlockSpec(memory_space=pltpu.VMEM)],
        out_specs=pl.BlockSpec(memory_space=pltpu.VMEM),
        scratch_shapes=[pltpu.VMEM((size, size), jnp.float32)],
        compiler_params=pltpu.CompilerParams(vmem_limit_bytes=32 * 1024 * 1024),
        cost_estimate=pl.CostEstimate(flops=size ** 3 * 60, bytes_accessed=8 * size * size, transcendentals=0),
    )(d)


def dot_t(a, b):
    return lax.dot_general(a, b, (((1,), (1,)), ((), ())), precision=HIGH, preferred_element_type=jnp.float32)


def shards(rows_count, panel, factor):
    own_cycles, row_block, width = panel.shape
    peers = width // row_block
    layer = lax.axis_index("layers")
    swap = [(0, 1), (1, 0)]
    target, diag_input = gather(rows_count // peers, peers, factor[0], panel[0])
    square = jnp.where(layer == 0, diag_input, 0.0) - dot_t(target, target)
    diag_block = square + lax.ppermute(square, "layers", swap)
    flat = factor.reshape(2, own_cycles * row_block, factor.shape[2])
    other = dot_t(lax.dynamic_index_in_dim(flat, 1 - layer, 0, False), target)
    from_other = lax.ppermute(other, "layers", swap)
    mine = dot_t(lax.dynamic_index_in_dim(flat, layer, 0, False), target)
    inverse = factor_inverse(diag_block)
    reduced = panel.reshape(-1, width) - (mine + from_other)
    return dot_t(reduced, inverse).reshape(panel.shape)


def solution(mesh):
    in_specs = (P("layers", "rows", None), P(None, "rows", "layers"))
    out_specs = P("layers", "rows", None)
    body = functools.partial(shards, mesh.shape["rows"])
    return jax.shard_map(body, mesh=mesh, in_specs=in_specs, out_specs=out_specs, check_vma=False)
```

```python
import functools
import jax
import jax.numpy as jnp
from jax import lax
from jax.experimental import pallas as pl
from jax.experimental.pallas import tpu as pltpu
from jax.sharding import PartitionSpec as P

MESH = pl.DeviceIdType.MESH
HIGH = lax.Precision.HIGH
TILE = 128
CHUNKS = 4


def gather_kernel(groups, peers, f_ref, p_ref, t_ref, d_ref, local_sem, z_send, z_recv, g_send, g_recv):
    row = lax.axis_index("rows")
    layer = lax.axis_index("layers")
    group = row // peers
    place = lax.rem(row, peers)
    base = group * peers
    has_prev = group > 0
    has_next = group < groups - 1
    prev = jnp.where(has_prev, row - peers, row)
    following = jnp.where(has_next, row + peers, row)
    heights = (f_ref.shape[0], p_ref.shape[0])
    part = heights[0] // CHUNKS
    wide = p_ref.shape[1] // peers

    barrier = pltpu.get_barrier_semaphore()

    def greet(who):
        pl.semaphore_signal(barrier, inc=1, device_id=(who, layer), device_id_type=MESH)

    for k in range(1, peers):
        greet(base + lax.rem(place + k, peers))

    @pl.when(has_prev)
    def _():
        greet(prev)

    @pl.when(has_next)
    def _():
        greet(following)

    pl.semaphore_wait(barrier, peers - 1 + has_prev.astype(jnp.int32) + has_next.astype(jnp.int32))

    def piece(a, dst, owner, c):
        if a == 0:
            return dst.at[pl.ds(pl.multiple_of(owner * heights[0] + c * part, part), part)]
        return dst.at[pl.ds(pl.multiple_of(owner * heights[1], heights[1]), heights[1]), pl.ds(c * wide, wide)]

    def chain(a, dst, c):
        return pltpu.make_async_remote_copy(
            src_ref=piece(a, dst, place, c), dst_ref=piece(a, dst, place, c),
            send_sem=z_send.at[a, c], recv_sem=z_recv.at[a, c],
            device_id=(following, layer), device_id_type=MESH)

    def spread(a, dst, c, k):
        to = base + lax.rem(place + k, peers)
        return pltpu.make_async_remote_copy(
            src_ref=piece(a, dst, place, c), dst_ref=piece(a, dst, place, c),
            send_sem=g_send.at[a, c, k], recv_sem=g_recv.at[a, c, k],
            device_id=(to, layer), device_id_type=MESH)

    def arrival(a, dst, c, k):
        src = lax.rem(place + peers - k, peers)
        return pltpu.make_async_remote_copy(
            src_ref=piece(a, dst, src, c), dst_ref=piece(a, dst, src, c),
            send_sem=g_send.at[a, c, k], recv_sem=g_recv.at[a, c, k],
            device_id=(base + src, layer), device_id_type=MESH)

    work = ((0, f_ref, t_ref), (1, p_ref, d_ref))
    steps = [(a, dst, c) for c in range(max(CHUNKS, peers))
             for a, dst in ((0, t_ref), (1, d_ref)) if c < (CHUNKS, peers)[a]]

    def when_used(a, owner, c, body):
        if a == 0:
            body()
        else:
            pl.when(c >= owner)(body)

    def own(a, src, dst):
        start = pl.multiple_of(place * heights[a], heights[a])
        return pltpu.make_async_copy(src, dst.at[pl.ds(start, heights[a])], local_sem.at[a])

    @pl.when(jnp.logical_not(has_prev))
    def _():
        for item in work:
            own(*item).start()
        for item in work:
            own(*item).wait()

    for a, dst, c in steps:
        def step(a=a, dst=dst, c=c):
            @pl.when(has_prev)
            def _():
                chain(a, dst, c).wait_recv()

            @pl.when(has_next)
            def _():
                chain(a, dst, c).start()

            for k in range(1, peers):
                spread(a, dst, c, k).start()

        when_used(a, place, c, step)

    for a, dst, c in steps:
        def finish(a=a, dst=dst, c=c):
            for k in range(1, peers):
                spread(a, dst, c, k).wait_send()

            @pl.when(has_next)
            def _():
                chain(a, dst, c).wait_send()

        when_used(a, place, c, finish)
        for k in range(1, peers):
            src = lax.rem(place + peers - k, peers)
            when_used(a, src, c, lambda a=a, dst=dst, c=c, k=k: arrival(a, dst, c, k).wait_recv())


def gather(groups, peers, f, p):
    rows, cols = f.shape
    out = jax.ShapeDtypeStruct((peers * rows, cols), f.dtype)
    out_p = jax.ShapeDtypeStruct((peers * p.shape[0], p.shape[1]), p.dtype)
    count = max(CHUNKS, peers)
    dma = pltpu.SemaphoreType.DMA
    return pl.pallas_call(
        functools.partial(gather_kernel, groups, peers),
        out_shape=(out, out_p),
        in_specs=[pl.BlockSpec(memory_space=pl.ANY)] * 2,
        out_specs=(pl.BlockSpec(memory_space=pl.ANY),) * 2,
        scratch_shapes=[dma((2,)), dma((2, count)), dma((2, count)),
                        dma((2, count, peers)), dma((2, count, peers))],
        compiler_params=pltpu.CompilerParams(collective_id=0, has_side_effects=True),
    )(f, p)


def split(x):
    hi = x.astype(jnp.bfloat16)
    return hi, (x - hi.astype(jnp.float32)).astype(jnp.bfloat16)


def dot3(a, b):
    a_hi, a_lo = a
    b_hi, b_lo = b
    mm = functools.partial(jnp.dot, preferred_element_type=jnp.float32)
    return mm(a_hi, b_hi) + (mm(a_hi, b_lo) + mm(a_lo, b_hi))


def small_inverse(e):
    low = [[None] * 8 for _ in range(8)]
    inv = [[None] * 8 for _ in range(8)]
    for j in range(8):
        root = lax.rsqrt(e[j][j])
        inv[j][j] = root
        for k in range(j):
            total = low[j][k] * inv[k][k]
            for m in range(k + 1, j):
                total = total + low[j][m] * inv[m][k]
            inv[j][k] = -(root * total)
        for i in range(j + 1, 8):
            low[i][j] = e[i][j] * root
        for i in range(j + 1, 8):
            for k in range(j + 1, i + 1):
                e[i][k] = e[i][k] - low[i][j] * low[k][j]
    return inv


def spread_row(tile, k):
    return jnp.broadcast_to(tile[k:k + 1, :], (8, TILE))


def combine(columns, tiles):
    total = columns[0] * tiles[0]
    for k in range(1, 8):
        total = total + columns[k] * tiles[k]
    return total


def base_inverse(block):
    n = TILE // 8
    sub = lax.broadcasted_iota(jnp.int32, (8, TILE), 0)
    lane = lax.broadcasted_iota(jnp.int32, (8, TILE), 1)
    is_row = [sub == k for k in range(8)]
    zero = jnp.zeros((8, TILE), jnp.float32)
    a = [block[8 * i:8 * i + 8, :] for i in range(n)]
    x = [jnp.where(lane == sub + 8 * i, 1.0, 0.0).astype(jnp.float32) for i in range(n)]
    for s in range(n):
        head = a[s]
        e = [[jnp.broadcast_to(head[i:i + 1, 8 * s + k:8 * s + k + 1], (8, TILE)) for k in range(i + 1)]
             for i in range(8)]
        inv = small_inverse(e)
        columns, rows = [], []
        for k in range(8):
            column, row = zero, zero
            for i in range(k, 8):
                column = jnp.where(is_row[i], inv[i][k], column)
            for i in range(k + 1):
                row = jnp.where(is_row[i], inv[k][i], row)
            columns.append(column)
            rows.append(row)
        xs = combine(columns, [spread_row(x[s], k) for k in range(8)])
        x[s] = xs
        if s == n - 1:
            break
        us = combine(columns, [spread_row(head, k) for k in range(8)])
        wa = combine(rows, [spread_row(us, k) for k in range(8)])
        wx = combine(rows, [spread_row(xs, k) for k in range(8)])
        wa = [spread_row(wa, k) for k in range(8)]
        wx = [spread_row(wx, k) for k in range(8)]
        for i in range(s + 1, n):
            cols = [jnp.broadcast_to(a[i][:, 8 * s + k:8 * s + k + 1], (8, TILE)) for k in range(8)]
            a[i] = a[i] - combine(cols, wa)
            x[i] = x[i] - combine(cols, wx)
    return jnp.concatenate(x, 0)


def inverse_kernel(d_ref, o_ref, m_ref):
    size = d_ref.shape[0]
    count = size // TILE
    m_ref[...] = d_ref[...]
    col_tile = lax.broadcasted_iota(jnp.int32, (TILE, size), 1) // TILE
    eye = (lax.broadcasted_iota(jnp.int32, (TILE, TILE), 0)
           == lax.broadcasted_iota(jnp.int32, (TILE, TILE), 1)).astype(jnp.float32)

    @pl.loop(0, count)
    def _(b):
        here = pl.ds(pl.multiple_of(b * TILE, TILE), TILE)
        inv = base_inverse(m_ref[here, here])
        m_ref[here, here] = eye
        u = dot3(split(inv), split(m_ref[here, :]))
        o_ref[here, :] = jnp.where(col_tile <= b, u, 0.0)
        m_ref[here, :] = u
        u_parts = split(u)

        @pl.loop(b + 1, count)
        def _(i):
            there = pl.ds(pl.multiple_of(i * TILE, TILE), TILE)
            left = m_ref[here, there].T
            old = jnp.where(col_tile == b, 0.0, m_ref[there, :])
            m_ref[there, :] = old - dot3(split(left), u_parts)


def factor_inverse(d):
    size = d.shape[0]
    return pl.pallas_call(
        inverse_kernel,
        out_shape=jax.ShapeDtypeStruct((size, size), jnp.float32),
        in_specs=[pl.BlockSpec(memory_space=pltpu.VMEM)],
        out_specs=pl.BlockSpec(memory_space=pltpu.VMEM),
        scratch_shapes=[pltpu.VMEM((size, size), jnp.float32)],
        compiler_params=pltpu.CompilerParams(vmem_limit_bytes=32 * 1024 * 1024),
        cost_estimate=pl.CostEstimate(flops=size ** 3 * 60, bytes_accessed=8 * size * size, transcendentals=0),
    )(d)


def dot_t(a, b):
    return lax.dot_general(a, b, (((1,), (1,)), ((), ())), precision=HIGH, preferred_element_type=jnp.float32)


def shards(rows_count, panel, factor):
    own_cycles, row_block, width = panel.shape
    peers = width // row_block
    layer = lax.axis_index("layers")
    swap = [(0, 1), (1, 0)]
    half = row_block // 2
    second = lax.ppermute(panel[0, half:], "layers", [(0, 1)])
    share = jnp.where(layer == 0, panel[0, :half], second)
    target, diag_share = gather(rows_count // peers, peers, factor[0], share)
    slot = lax.broadcasted_iota(jnp.int32, (1, 2, 1, 1), 1) == layer
    diag_input = jnp.where(slot, diag_share.reshape(peers, 1, half, width), 0.0).reshape(width, width)
    square = diag_input - dot_t(target, target)
    diag_block = square + lax.ppermute(square, "layers", swap)
    flat = factor.reshape(2, own_cycles * row_block, factor.shape[2])
    other = dot_t(lax.dynamic_index_in_dim(flat, 1 - layer, 0, False), target)
    from_other = lax.ppermute(other, "layers", swap)
    mine = dot_t(lax.dynamic_index_in_dim(flat, layer, 0, False), target)
    inverse = factor_inverse(diag_block)
    reduced = panel.reshape(-1, width) - (mine + from_other)
    return dot_t(reduced, inverse).reshape(panel.shape)


def solution(mesh):
    in_specs = (P("layers", "rows", None), P(None, "rows", "layers"))
    out_specs = P("layers", "rows", None)
    body = functools.partial(shards, mesh.shape["rows"])
    return jax.shard_map(body, mesh=mesh, in_specs=in_specs, out_specs=out_specs, check_vma=False)
```

```python
import functools
import jax
import jax.numpy as jnp
from jax import lax
from jax.experimental import pallas as pl
from jax.experimental.pallas import tpu as pltpu
from jax.sharding import PartitionSpec as P

MESH = pl.DeviceIdType.MESH
HIGH = lax.Precision.HIGH
TILE = 128
CHUNKS = 8
LAG = 2


def gather_kernel(groups, peers, f_ref, p_ref, t_ref, d_ref, local_sem, z_send, z_recv, g_send, g_recv):
    row = lax.axis_index("rows")
    layer = lax.axis_index("layers")
    group = row // peers
    place = lax.rem(row, peers)
    base = group * peers
    has_prev = group > 0
    has_next = group < groups - 1
    prev = jnp.where(has_prev, row - peers, row)
    following = jnp.where(has_next, row + peers, row)
    heights = (f_ref.shape[0], p_ref.shape[0])
    part = heights[0] // CHUNKS
    wide = p_ref.shape[1] // peers

    barrier = pltpu.get_barrier_semaphore()

    def greet(who):
        pl.semaphore_signal(barrier, inc=1, device_id=(who, layer), device_id_type=MESH)

    beside = (place + 1 - 2 * lax.rem(place, 2), lax.rem(place + 2, peers))
    across = lax.rem(beside[0] + 2, peers)
    for who in beside:
        greet(base + who)

    @pl.when(has_prev)
    def _():
        greet(prev)

    @pl.when(has_next)
    def _():
        greet(following)

    pl.semaphore_wait(barrier, 2 + has_prev.astype(jnp.int32) + has_next.astype(jnp.int32))

    def piece(a, dst, owner, c):
        if a == 0:
            return dst.at[pl.ds(pl.multiple_of(owner * heights[0] + c * part, part), part)]
        return dst.at[pl.ds(pl.multiple_of(owner * heights[1], heights[1]), heights[1]), pl.ds(c * wide, wide)]

    def chain(a, dst, c):
        return pltpu.make_async_remote_copy(
            src_ref=piece(a, dst, place, c), dst_ref=piece(a, dst, place, c),
            send_sem=z_send.at[a, c], recv_sem=z_recv.at[a, c],
            device_id=(following, layer), device_id_type=MESH)

    def send(a, dst, c, owner, to, k):
        return pltpu.make_async_remote_copy(
            src_ref=piece(a, dst, owner, c), dst_ref=piece(a, dst, owner, c),
            send_sem=g_send.at[a, c, k], recv_sem=g_recv.at[a, c, k],
            device_id=(base + to, layer), device_id_type=MESH)

    work = ((0, f_ref, t_ref), (1, p_ref, d_ref))
    steps = [(a, dst, c) for c in range(max(CHUNKS, peers))
             for a, dst in ((0, t_ref), (1, d_ref)) if c < (CHUNKS, peers)[a]]

    def when_used(a, owner, c, body):
        if a == 0:
            body()
        else:
            pl.when(c >= owner)(body)

    def own(a, src, dst):
        start = pl.multiple_of(place * heights[a], heights[a])
        return pltpu.make_async_copy(src, dst.at[pl.ds(start, heights[a])], local_sem.at[a])

    @pl.when(jnp.logical_not(has_prev))
    def _():
        for item in work:
            own(*item).start()
        for item in work:
            own(*item).wait()

    def issue(a, dst, c):
        def body():
            @pl.when(has_prev)
            def _():
                chain(a, dst, c).wait_recv()

            @pl.when(has_next)
            def _():
                chain(a, dst, c).start()

            for k in range(2):
                send(a, dst, c, place, beside[k], k).start()

        when_used(a, place, c, body)

    def forward(a, dst, c):
        for k in range(2):
            def body(k=k):
                send(a, dst, c, beside[k], beside[k], k).wait_recv()
                if c % 2 == k:
                    send(a, dst, c, beside[k], beside[1 - k], 2).start()

            when_used(a, beside[k], c, body)

    def finish(a, dst, c):
        def own_sent():
            for k in range(2):
                send(a, dst, c, place, beside[k], k).wait_send()

            @pl.when(has_next)
            def _():
                chain(a, dst, c).wait_send()

        when_used(a, place, c, own_sent)
        k = c % 2
        when_used(a, beside[k], c, lambda: send(a, dst, c, beside[k], beside[1 - k], 2).wait_send())
        when_used(a, across, c, lambda: send(a, dst, c, across, across, 2).wait_recv())

    for i in range(len(steps) + LAG):
        if i < len(steps):
            issue(*steps[i])
        if i >= LAG:
            forward(*steps[i - LAG])
    for item in steps:
        finish(*item)


def gather(groups, peers, f, p):
    rows, cols = f.shape
    out = jax.ShapeDtypeStruct((peers * rows, cols), f.dtype)
    out_p = jax.ShapeDtypeStruct((peers * p.shape[0], p.shape[1]), p.dtype)
    count = max(CHUNKS, peers)
    dma = pltpu.SemaphoreType.DMA
    return pl.pallas_call(
        functools.partial(gather_kernel, groups, peers),
        out_shape=(out, out_p),
        in_specs=[pl.BlockSpec(memory_space=pl.ANY)] * 2,
        out_specs=(pl.BlockSpec(memory_space=pl.ANY),) * 2,
        scratch_shapes=[dma((2,)), dma((2, count)), dma((2, count)),
                        dma((2, count, peers)), dma((2, count, peers))],
        compiler_params=pltpu.CompilerParams(collective_id=0, has_side_effects=True),
    )(f, p)


def split(x):
    hi = x.astype(jnp.bfloat16)
    return hi, (x - hi.astype(jnp.float32)).astype(jnp.bfloat16)


def dot3(a, b):
    a_hi, a_lo = a
    b_hi, b_lo = b
    mm = functools.partial(jnp.dot, preferred_element_type=jnp.float32)
    return mm(a_hi, b_hi) + (mm(a_hi, b_lo) + mm(a_lo, b_hi))


def small_inverse(e):
    low = [[None] * 8 for _ in range(8)]
    inv = [[None] * 8 for _ in range(8)]
    for j in range(8):
        root = lax.rsqrt(e[j][j])
        inv[j][j] = root
        for k in range(j):
            total = low[j][k] * inv[k][k]
            for m in range(k + 1, j):
                total = total + low[j][m] * inv[m][k]
            inv[j][k] = -(root * total)
        for i in range(j + 1, 8):
            low[i][j] = e[i][j] * root
        for i in range(j + 1, 8):
            for k in range(j + 1, i + 1):
                e[i][k] = e[i][k] - low[i][j] * low[k][j]
    return inv


def spread_row(tile, k):
    return jnp.broadcast_to(tile[k:k + 1, :], (8, TILE))


def combine(columns, tiles):
    total = columns[0] * tiles[0]
    for k in range(1, 8):
        total = total + columns[k] * tiles[k]
    return total


def base_inverse(block):
    n = TILE // 8
    sub = lax.broadcasted_iota(jnp.int32, (8, TILE), 0)
    lane = lax.broadcasted_iota(jnp.int32, (8, TILE), 1)
    is_row = [sub == k for k in range(8)]
    zero = jnp.zeros((8, TILE), jnp.float32)
    a = [block[8 * i:8 * i + 8, :] for i in range(n)]
    x = [jnp.where(lane == sub + 8 * i, 1.0, 0.0).astype(jnp.float32) for i in range(n)]
    for s in range(n):
        head = a[s]
        e = [[jnp.broadcast_to(head[i:i + 1, 8 * s + k:8 * s + k + 1], (8, TILE)) for k in range(i + 1)]
             for i in range(8)]
        inv = small_inverse(e)
        columns, rows = [], []
        for k in range(8):
            column, row = zero, zero
            for i in range(k, 8):
                column = jnp.where(is_row[i], inv[i][k], column)
            for i in range(k + 1):
                row = jnp.where(is_row[i], inv[k][i], row)
            columns.append(column)
            rows.append(row)
        xs = combine(columns, [spread_row(x[s], k) for k in range(8)])
        x[s] = xs
        if s == n - 1:
            break
        us = combine(columns, [spread_row(head, k) for k in range(8)])
        wa = combine(rows, [spread_row(us, k) for k in range(8)])
        wx = combine(rows, [spread_row(xs, k) for k in range(8)])
        wa = [spread_row(wa, k) for k in range(8)]
        wx = [spread_row(wx, k) for k in range(8)]
        for i in range(s + 1, n):
            cols = [jnp.broadcast_to(a[i][:, 8 * s + k:8 * s + k + 1], (8, TILE)) for k in range(8)]
            a[i] = a[i] - combine(cols, wa)
            x[i] = x[i] - combine(cols, wx)
    return jnp.concatenate(x, 0)


def inverse_kernel(d_ref, o_ref, m_ref):
    size = d_ref.shape[0]
    count = size // TILE
    m_ref[...] = d_ref[...]
    col_tile = lax.broadcasted_iota(jnp.int32, (TILE, size), 1) // TILE
    eye = (lax.broadcasted_iota(jnp.int32, (TILE, TILE), 0)
           == lax.broadcasted_iota(jnp.int32, (TILE, TILE), 1)).astype(jnp.float32)

    @pl.loop(0, count)
    def _(b):
        here = pl.ds(pl.multiple_of(b * TILE, TILE), TILE)
        inv = base_inverse(m_ref[here, here])
        m_ref[here, here] = eye
        u = dot3(split(inv), split(m_ref[here, :]))
        o_ref[here, :] = jnp.where(col_tile <= b, u, 0.0)
        m_ref[here, :] = u
        u_parts = split(u)

        @pl.loop(b + 1, count)
        def _(i):
            there = pl.ds(pl.multiple_of(i * TILE, TILE), TILE)
            left = m_ref[here, there].T
            old = jnp.where(col_tile == b, 0.0, m_ref[there, :])
            m_ref[there, :] = old - dot3(split(left), u_parts)


def factor_inverse(d):
    size = d.shape[0]
    return pl.pallas_call(
        inverse_kernel,
        out_shape=jax.ShapeDtypeStruct((size, size), jnp.float32),
        in_specs=[pl.BlockSpec(memory_space=pltpu.VMEM)],
        out_specs=pl.BlockSpec(memory_space=pltpu.VMEM),
        scratch_shapes=[pltpu.VMEM((size, size), jnp.float32)],
        compiler_params=pltpu.CompilerParams(vmem_limit_bytes=32 * 1024 * 1024),
        cost_estimate=pl.CostEstimate(flops=size ** 3 * 60, bytes_accessed=8 * size * size, transcendentals=0),
    )(d)


def dot_t(a, b):
    return lax.dot_general(a, b, (((1,), (1,)), ((), ())), precision=HIGH, preferred_element_type=jnp.float32)


def shards(rows_count, panel, factor):
    own_cycles, row_block, width = panel.shape
    peers = width // row_block
    layer = lax.axis_index("layers")
    swap = [(0, 1), (1, 0)]
    half = row_block // 2
    second = lax.ppermute(panel[0, half:], "layers", [(0, 1)])
    share = jnp.where(layer == 0, panel[0, :half], second)
    target, diag_share = gather(rows_count // peers, peers, factor[0], share)
    slot = lax.broadcasted_iota(jnp.int32, (1, 2, 1, 1), 1) == layer
    diag_input = jnp.where(slot, diag_share.reshape(peers, 1, half, width), 0.0).reshape(width, width)
    square = diag_input - dot_t(target, target)
    diag_block = square + lax.ppermute(square, "layers", swap)
    flat = factor.reshape(2, own_cycles * row_block, factor.shape[2])
    other = dot_t(lax.dynamic_index_in_dim(flat, 1 - layer, 0, False), target)
    from_other = lax.ppermute(other, "layers", swap)
    mine = dot_t(lax.dynamic_index_in_dim(flat, layer, 0, False), target)
    inverse = factor_inverse(diag_block)
    reduced = panel.reshape(-1, width) - (mine + from_other)
    return dot_t(reduced, inverse).reshape(panel.shape)


def solution(mesh):
    in_specs = (P("layers", "rows", None), P(None, "rows", "layers"))
    out_specs = P("layers", "rows", None)
    body = functools.partial(shards, mesh.shape["rows"])
    return jax.shard_map(body, mesh=mesh, in_specs=in_specs, out_specs=out_specs, check_vma=False)
```

```python
import functools
import jax
import jax.numpy as jnp
from jax import lax
from jax.experimental import pallas as pl
from jax.experimental.pallas import tpu as pltpu
from jax.sharding import PartitionSpec as P

MESH = pl.DeviceIdType.MESH
HIGH = lax.Precision.HIGH
TILE = 128
CHUNKS = 16
LAG = 2


def gather_kernel(groups, peers, f_ref, p_ref, t_ref, d_ref, local_sem, z_send, z_recv, g_send, g_recv):
    row = lax.axis_index("rows")
    layer = lax.axis_index("layers")
    group = row // peers
    place = lax.rem(row, peers)
    base = group * peers
    has_prev = group > 0
    has_next = group < groups - 1
    prev = jnp.where(has_prev, row - peers, row)
    following = jnp.where(has_next, row + peers, row)
    heights = (f_ref.shape[1], p_ref.shape[0])
    part = heights[0] // CHUNKS
    wide = p_ref.shape[1] // peers

    barrier = pltpu.get_barrier_semaphore()

    def greet(who):
        pl.semaphore_signal(barrier, inc=1, device_id=(who, layer), device_id_type=MESH)

    beside = (place + 1 - 2 * lax.rem(place, 2), lax.rem(place + 2, peers))
    across = lax.rem(beside[0] + 2, peers)
    for who in beside:
        greet(base + who)

    @pl.when(has_prev)
    def _():
        greet(prev)

    @pl.when(has_next)
    def _():
        greet(following)

    pl.semaphore_wait(barrier, 2 + has_prev.astype(jnp.int32) + has_next.astype(jnp.int32))

    def piece(a, dst, owner, c):
        if a == 0:
            return dst.at[pl.ds(pl.multiple_of(owner * heights[0] + c * part, part), part)]
        return dst.at[pl.ds(pl.multiple_of(owner * heights[1], heights[1]), heights[1]), pl.ds(c * wide, wide)]

    def chain(a, dst, c):
        return pltpu.make_async_remote_copy(
            src_ref=piece(a, dst, place, c), dst_ref=piece(a, dst, place, c),
            send_sem=z_send.at[a, c], recv_sem=z_recv.at[a, c],
            device_id=(following, layer), device_id_type=MESH)

    def send(a, dst, c, owner, to, k):
        return pltpu.make_async_remote_copy(
            src_ref=piece(a, dst, owner, c), dst_ref=piece(a, dst, owner, c),
            send_sem=g_send.at[a, c, k], recv_sem=g_recv.at[a, c, k],
            device_id=(base + to, layer), device_id_type=MESH)

    work = ((0, f_ref.at[0], t_ref), (1, p_ref, d_ref))
    steps = [(a, dst, c) for c in range(max(CHUNKS, peers))
             for a, dst in ((0, t_ref), (1, d_ref)) if c < (CHUNKS, peers)[a]]

    def when_used(a, owner, c, body):
        if a == 0:
            body()
        else:
            pl.when(c >= owner)(body)

    def own(a, src, dst):
        start = pl.multiple_of(place * heights[a], heights[a])
        return pltpu.make_async_copy(src, dst.at[pl.ds(start, heights[a])], local_sem.at[a])

    @pl.when(jnp.logical_not(has_prev))
    def _():
        for item in work:
            own(*item).start()
        for item in work:
            own(*item).wait()

    def issue(a, dst, c):
        def body():
            @pl.when(has_prev)
            def _():
                chain(a, dst, c).wait_recv()

            @pl.when(has_next)
            def _():
                chain(a, dst, c).start()

            for k in range(2):
                send(a, dst, c, place, beside[k], k).start()

        when_used(a, place, c, body)

    def forward(a, dst, c):
        for k in range(2):
            def body(k=k):
                send(a, dst, c, beside[k], beside[k], k).wait_recv()
                if c % 2 == k:
                    send(a, dst, c, beside[k], beside[1 - k], 2).start()

            when_used(a, beside[k], c, body)

    def finish(a, dst, c):
        def own_sent():
            for k in range(2):
                send(a, dst, c, place, beside[k], k).wait_send()

            @pl.when(has_next)
            def _():
                chain(a, dst, c).wait_send()

        when_used(a, place, c, own_sent)
        k = c % 2
        when_used(a, beside[k], c, lambda: send(a, dst, c, beside[k], beside[1 - k], 2).wait_send())
        when_used(a, across, c, lambda: send(a, dst, c, across, across, 2).wait_recv())

    for i in range(len(steps) + LAG):
        if i < len(steps):
            issue(*steps[i])
        if i >= LAG:
            forward(*steps[i - LAG])
    for item in steps:
        finish(*item)


def gather(groups, peers, f, p):
    rows, cols = f.shape[1:]
    out = jax.ShapeDtypeStruct((peers * rows, cols), f.dtype)
    out_p = jax.ShapeDtypeStruct((peers * p.shape[0], p.shape[1]), p.dtype)
    count = max(CHUNKS, peers)
    dma = pltpu.SemaphoreType.DMA
    return pl.pallas_call(
        functools.partial(gather_kernel, groups, peers),
        out_shape=(out, out_p),
        in_specs=[pl.BlockSpec(memory_space=pl.ANY)] * 2,
        out_specs=(pl.BlockSpec(memory_space=pl.ANY),) * 2,
        scratch_shapes=[dma((2,)), dma((2, count)), dma((2, count)),
                        dma((2, count, peers)), dma((2, count, peers))],
        compiler_params=pltpu.CompilerParams(collective_id=0, has_side_effects=True),
    )(f, p)


def split(x):
    hi = x.astype(jnp.bfloat16)
    return hi, (x - hi.astype(jnp.float32)).astype(jnp.bfloat16)


def dot3(a, b):
    a_hi, a_lo = a
    b_hi, b_lo = b
    mm = functools.partial(jnp.dot, preferred_element_type=jnp.float32)
    return mm(a_hi, b_hi) + (mm(a_hi, b_lo) + mm(a_lo, b_hi))


def small_inverse(e):
    low = [[None] * 8 for _ in range(8)]
    inv = [[None] * 8 for _ in range(8)]
    for j in range(8):
        root = lax.rsqrt(e[j][j])
        inv[j][j] = root
        for k in range(j):
            total = low[j][k] * inv[k][k]
            for m in range(k + 1, j):
                total = total + low[j][m] * inv[m][k]
            inv[j][k] = -(root * total)
        for i in range(j + 1, 8):
            low[i][j] = e[i][j] * root
        for i in range(j + 1, 8):
            for k in range(j + 1, i + 1):
                e[i][k] = e[i][k] - low[i][j] * low[k][j]
    return inv


def spread_row(tile, k):
    return jnp.broadcast_to(tile[k:k + 1, :], (8, TILE))


def combine(columns, tiles):
    total = columns[0] * tiles[0]
    for k in range(1, 8):
        total = total + columns[k] * tiles[k]
    return total


def base_inverse(block):
    n = TILE // 8
    sub = lax.broadcasted_iota(jnp.int32, (8, TILE), 0)
    lane = lax.broadcasted_iota(jnp.int32, (8, TILE), 1)
    is_row = [sub == k for k in range(8)]
    zero = jnp.zeros((8, TILE), jnp.float32)
    a = [block[8 * i:8 * i + 8, :] for i in range(n)]
    x = [jnp.where(lane == sub + 8 * i, 1.0, 0.0).astype(jnp.float32) for i in range(n)]
    for s in range(n):
        head = a[s]
        e = [[jnp.broadcast_to(head[i:i + 1, 8 * s + k:8 * s + k + 1], (8, TILE)) for k in range(i + 1)]
             for i in range(8)]
        inv = small_inverse(e)
        columns, rows = [], []
        for k in range(8):
            column, row = zero, zero
            for i in range(k, 8):
                column = jnp.where(is_row[i], inv[i][k], column)
            for i in range(k + 1):
                row = jnp.where(is_row[i], inv[k][i], row)
            columns.append(column)
            rows.append(row)
        xs = combine(columns, [spread_row(x[s], k) for k in range(8)])
        x[s] = xs
        if s == n - 1:
            break
        us = combine(columns, [spread_row(head, k) for k in range(8)])
        wa = combine(rows, [spread_row(us, k) for k in range(8)])
        wx = combine(rows, [spread_row(xs, k) for k in range(8)])
        wa = [spread_row(wa, k) for k in range(8)]
        wx = [spread_row(wx, k) for k in range(8)]
        for i in range(s + 1, n):
            cols = [jnp.broadcast_to(a[i][:, 8 * s + k:8 * s + k + 1], (8, TILE)) for k in range(8)]
            a[i] = a[i] - combine(cols, wa)
            x[i] = x[i] - combine(cols, wx)
    return jnp.concatenate(x, 0)


def inverse_kernel(d_ref, e_ref, o_ref, m_ref):
    size = d_ref.shape[0]
    count = size // TILE
    m_ref[...] = d_ref[...] + e_ref[...]
    col_tile = lax.broadcasted_iota(jnp.int32, (TILE, size), 1) // TILE
    eye = (lax.broadcasted_iota(jnp.int32, (TILE, TILE), 0)
           == lax.broadcasted_iota(jnp.int32, (TILE, TILE), 1)).astype(jnp.float32)

    @pl.loop(0, count)
    def _(b):
        here = pl.ds(pl.multiple_of(b * TILE, TILE), TILE)
        inv = base_inverse(m_ref[here, here])
        m_ref[here, here] = eye
        u = dot3(split(inv), split(m_ref[here, :]))
        o_ref[here, :] = jnp.where(col_tile <= b, u, 0.0)
        m_ref[here, :] = u
        u_parts = split(u)

        @pl.loop(b + 1, count)
        def _(i):
            there = pl.ds(pl.multiple_of(i * TILE, TILE), TILE)
            left = m_ref[here, there].T
            old = jnp.where(col_tile == b, 0.0, m_ref[there, :])
            m_ref[there, :] = old - dot3(split(left), u_parts)


def factor_inverse(d, e):
    size = d.shape[0]
    return pl.pallas_call(
        inverse_kernel,
        out_shape=jax.ShapeDtypeStruct((size, size), jnp.float32),
        in_specs=[pl.BlockSpec(memory_space=pltpu.VMEM)] * 2,
        out_specs=pl.BlockSpec(memory_space=pltpu.VMEM),
        scratch_shapes=[pltpu.VMEM((size, size), jnp.float32)],
        compiler_params=pltpu.CompilerParams(vmem_limit_bytes=32 * 1024 * 1024),
        cost_estimate=pl.CostEstimate(flops=size ** 3 * 60, bytes_accessed=8 * size * size, transcendentals=0),
    )(d, e)


def dot_t(a, b):
    return lax.dot_general(a, b, (((1,), (1,)), ((), ())), precision=HIGH, preferred_element_type=jnp.float32)


def shards(rows_count, panel, factor):
    own_cycles, row_block, width = panel.shape
    peers = width // row_block
    layer = lax.axis_index("layers")
    swap = [(0, 1), (1, 0)]
    half = row_block // 2
    second = lax.ppermute(panel[0, half:], "layers", [(0, 1)])
    share = jnp.where(layer == 0, panel[0, :half], second)
    target, diag_share = gather(rows_count // peers, peers, factor, share)
    slot = lax.broadcasted_iota(jnp.int32, (1, 2, 1, 1), 1) == layer
    diag_input = jnp.where(slot, diag_share.reshape(peers, 1, half, width), 0.0).reshape(width, width)
    square = diag_input - dot_t(target, target)
    from_square = lax.ppermute(square, "layers", swap)
    flat = factor.reshape(2, own_cycles * row_block, factor.shape[2])
    other = dot_t(lax.dynamic_index_in_dim(flat, 1 - layer, 0, False), target)
    from_other = lax.ppermute(other, "layers", swap)
    mine = dot_t(lax.dynamic_index_in_dim(flat, layer, 0, False), target)
    inverse = factor_inverse(square, from_square)
    reduced = panel.reshape(-1, width) - (mine + from_other)
    return dot_t(reduced, inverse).reshape(panel.shape)


def solution(mesh):
    in_specs = (P("layers", "rows", None), P(None, "rows", "layers"))
    out_specs = P("layers", "rows", None)
    body = functools.partial(shards, mesh.shape["rows"])
    return jax.shard_map(body, mesh=mesh, in_specs=in_specs, out_specs=out_specs, check_vma=False)
```
